32 devices in a mesh: groups: 2 (over x), fsdp: 16 (over z, y, core).
Axes of the slice: x: 2, y: 2, z: 4, core: 2. Of those that a mesh axis runs over, the one named last changes fastest.
Arguments:
- step_hidden: bfloat16 [16384, 4096], P(('groups', 'fsdp')), parts along dimension 0, may hold values from -6 to 6
- prm_cache: bfloat16 [512, 128, 1024], P(('groups', 'fsdp')), parts along dimension 0, may hold values from -256 to 256
- lengths: int32 [512], P(('groups', 'fsdp')), parts along dimension 0, may hold values from 32 to 128
- w_query: bfloat16 [4096, 2048], P('fsdp'), may hold values from -0.09375 to 0.09375
- w_keyval: bfloat16 [4096, 1024], P('fsdp'), may hold values from -0.09375 to 0.09375
- reward_head: float32 [2048], replicated, may hold values from -0.125 to 0.125
- placement: int32 [512], P('groups'), parts along dimension 0, may hold values from 0 to 255, each once
- parents: int32 [512], P('groups'), parts along dimension 0, may hold values from 0 to 255, as said below
- page_table: int32 [512, 2], P(('groups', 'fsdp')), parts along dimension 0, may hold values from 0 to 31, as said below
- policy_pool: bfloat16 [1024, 64, 1024], P(('groups', 'fsdp')), parts along dimension 0, may hold values from -6 to 6
- new_query: bfloat16 [512, 2, 2048], P(('groups', 'fsdp')), parts along dimension 0, may hold values from -180 to 180
- new_keyval: bfloat16 [512, 2, 1024], P(('groups', 'fsdp')), parts along dimension 0, may hold values from -6 to 6
Outputs:
- rewards: float32 [512], P(('groups', 'fsdp')), parts along dimension 0
- decoded: bfloat16 [512, 2, 2048], P(('groups', 'fsdp')), parts along dimension 0
The draws below stay inside these ranges and needn't reach their ends.
There are 2 independent parts, one for each index of `groups`. The reference program is written for one: setup_inputs(seed, part) draws one part's arguments, and reference() takes and returns one part's arrays. A program takes and returns all parts, laid end to end along the dimension named above; an argument that names none is the same for every part. Nothing has to cross between parts.
Inputs may be any that keep to these rules, and one draw needn't show every extreme that they name: The rows that one device's slots name in page_table cover each of that device's 16 * 2 pool rows once. The 16 children d * 16 to d * 16 + 15 of one device have parent slots on distinct devices (parents[c] // 16); in every draw some device holds the parent of one child of every device.
All inputs are finite; a program needn't handle non-finite values.
Results may differ from the reference program's by a relative error of at most 0.012.
Values may be sent and summed in bfloat16 or wider, within the bound.
A program may use at most 192 MiB of HBM per device.

```python
import math
import jax
import jax.numpy as jnp
from jax import lax

D = 4096
HQ = 16
HD = 128
B_DEV = 16
CTX = 128
STEP = 32
PAGE = 64
NEW = 2
BEAMS = 256
QW = 2048
KVW = 512
PPB = 2


def draw_page_table(key, part):
    key = jax.random.fold_in(key, 7)
    device_count = BEAMS // B_DEV
    pool_size = B_DEV * PPB
    key_list = jax.random.split(key, device_count)
    orderings = jax.vmap(lambda single: jax.random.permutation(single, pool_size))(key_list)
    return orderings.reshape(BEAMS, PPB).astype(jnp.int32)


def draw_parents(key, part):
    key = jax.random.fold_in(key, 11)
    device_count = BEAMS // B_DEV
    key_list = jax.random.split(key, 5)
    hot_device = jax.random.randint(key_list[0], (), 0, device_count)
    ranking = jax.random.permutation(key_list[1], device_count)
    favour = 16384 // (ranking + 4)
    raw_score = jax.random.randint(key_list[2], (device_count, device_count), 0, favour[None, :])
    column = jnp.arange(device_count, dtype=jnp.int32)
    row_index = column[:, None]
    ranked = raw_score * device_count + column[None, :]
    far_end = (row_index == 0) & (column[None, :] == device_count - 1)
    near_end = (row_index == 1) & (column[None, :] == 0)
    ranked = jnp.where(far_end | near_end, 2 ** 29, ranked)
    ranked = jnp.where(column[None, :] == hot_device, 2 ** 30, ranked)
    chosen = lax.top_k(ranked, B_DEV)[1].astype(jnp.int32)
    inner = jax.random.randint(key_list[3], (device_count, B_DEV), 0, B_DEV)
    inner = jnp.where((row_index == 0) & (chosen == device_count - 1), B_DEV - 1, inner)
    inner = jnp.where((row_index == 1) & (chosen == 0), 0, inner)
    slots = chosen * B_DEV + inner
    shuffle = jax.random.randint(key_list[4], (device_count, B_DEV), 0, 65536) * B_DEV + jnp.arange(B_DEV, dtype=jnp.int32)[None, :]
    order = jnp.argsort(shuffle, axis=1)
    slots = jnp.take_along_axis(slots, order, axis=1)
    return slots.reshape(BEAMS).astype(jnp.int32)


def draw_prm_cache(key, part):
    key = jax.random.fold_in(key, 3)
    key_list = jax.random.split(key, 4)
    shape = (BEAMS, CTX, KVW)
    key_base = jnp.clip(jax.random.normal(key_list[0], shape, jnp.float32), -6.0, 6.0)
    noise = jnp.clip(jax.random.normal(key_list[1], shape, jnp.float32), -6.0, 6.0)
    shared = jnp.clip(jax.random.normal(key_list[2], (BEAMS, 1, KVW), jnp.float32), -3.0, 3.0)
    low_scale = 0.6
    high_scale = 1.6
    key_scale = jnp.exp(jax.random.uniform(key_list[3], (BEAMS, CTX, 1), jnp.float32, math.log(low_scale), math.log(high_scale)))
    keys = key_base * key_scale
    values = shared + noise
    return jnp.concatenate([keys, values], axis=2).astype(jnp.bfloat16)


def draw_new_query(key, part):
    key = jax.random.fold_in(key, 5)
    key_list = jax.random.split(key, 2)
    shape = (BEAMS, NEW, HQ, HD)
    base = jnp.clip(jax.random.normal(key_list[0], shape, jnp.float32), -6.0, 6.0)
    high_scale = 2.5
    head_scale = jnp.exp(jax.random.uniform(key_list[1], (BEAMS, NEW, HQ, 1), jnp.float32, 0.0, math.log(high_scale)))
    return (base * head_scale).reshape(BEAMS, NEW, HQ * HD).astype(jnp.bfloat16)


def plant(array, rng, low, top_value):
    shape = array.shape
    spot = [jax.random.randint(jax.random.fold_in(rng, axis), (), 0, shape[axis]) for axis in range(len(shape))]
    array = array.at[tuple(spot)].set(low)
    longest = shape.index(max(shape))
    spot[longest] = (spot[longest] + 1) % shape[longest]
    return array.at[tuple(spot)].set(top_value)


def block_scale(rng, dims, shards, low, high):
    gain, own = 1.0, jax.random.fold_in(rng, 6)
    for dim, blocks in shards:
        steps = jnp.exp(jax.random.uniform(jax.random.fold_in(own, dim), (blocks,), jnp.float32, low / len(shards), high / len(shards)))
        gain = gain * jnp.repeat(steps, dims[dim] // blocks).reshape([-1 if axis == dim else 1 for axis in range(len(dims))])
    return gain


def normal_values(own_key, dims, spread, most, cuts=(), held_as=jnp.bfloat16):
    factor_of = block_scale(own_key, dims, cuts, -0.22, 0.18) if cuts else 1.0
    entries = jax.random.normal(own_key, dims, jnp.float32) * spread * factor_of
    return jnp.minimum(jnp.maximum(entries, -most), most).astype(held_as)


def setup_inputs(seed: int = 0, part: int = 0) -> dict:
    key_of = jax.random.split(jax.random.key(seed), 13)
    own_keys = jax.random.split(jax.random.fold_in(key_of[12], part), 13)
    return {
        "step_hidden": normal_values(own_keys[0], (BEAMS * STEP, D), 1.0, 6.0, ((0, 16),)),
        "prm_cache": draw_prm_cache(jax.random.fold_in(jax.random.fold_in(key_of[12], part), 71), part),
        "lengths": plant(jax.random.randint(own_keys[2], (BEAMS,), CTX // 4, CTX + 1), jax.random.fold_in(own_keys[2], 1), CTX // 4, CTX).astype(jnp.int32),
        "w_query": normal_values(key_of[3], (D, QW), D ** -0.5, 0.09375, ((0, 16),)),
        "w_keyval": normal_values(key_of[4], (D, 2 * KVW), D ** -0.5, 0.09375, ((0, 16),)),
        "reward_head": normal_values(key_of[5], (QW,), QW ** -0.5, 0.125, (), jnp.float32),
        "placement": jax.random.permutation(own_keys[6], BEAMS).astype(jnp.int32),
        "parents": draw_parents(jax.random.fold_in(jax.random.fold_in(key_of[12], part), 71), part),
        "page_table": draw_page_table(jax.random.fold_in(jax.random.fold_in(key_of[12], part), 71), part),
        "policy_pool": normal_values(own_keys[9], (BEAMS * PPB, PAGE, 2 * KVW), 1.0, 6.0, ((0, 16),)),
        "new_query": draw_new_query(jax.random.fold_in(jax.random.fold_in(key_of[12], part), 71), part),
        "new_keyval": normal_values(own_keys[11], (BEAMS, NEW, 2 * KVW), 1.0, 6.0, ((0, 16),)),
    }


def rms_rows(states):
    widened = states.astype(jnp.float32)
    scale_row = lax.rsqrt(lax.optimization_barrier(jnp.mean(widened * widened, axis=-1, keepdims=True)) + 1e-05)
    return (widened * scale_row).astype(jnp.bfloat16)

def rounded(weights):
    narrow = lax.optimization_barrier(weights.astype(jnp.bfloat16))
    return narrow.astype(jnp.float32)

def score_steps(query_vec, cache_rows, fresh_keyval, lengths):
    beam_count = query_vec.shape[0]
    cache_len = cache_rows.shape[1]
    kv_width = cache_rows.shape[2] // 2
    kv_heads = kv_width // HD
    group_size = query_vec.shape[1] // kv_width
    joined = jnp.concatenate([cache_rows, fresh_keyval], axis=1)
    span_len = joined.shape[1]
    key_heads = joined[:, :, :kv_width].astype(jnp.float32).reshape(beam_count, span_len, kv_heads, HD)
    value_heads = joined[:, :, kv_width:].astype(jnp.float32).reshape(beam_count, span_len, kv_heads, HD)
    query_heads = query_vec.astype(jnp.float32).reshape(beam_count, kv_heads, group_size, HD)
    scores = jnp.einsum('bgrd,blgd->bgrl', query_heads, key_heads) / math.sqrt(HD)
    position = jnp.arange(span_len, dtype=jnp.int32)
    usable = (position[None, :] < lengths[:, None]) | (position[None, :] >= cache_len)
    usable = usable[:, None, None, :]
    scores = jnp.where(usable, scores, -1e+30)
    peak_val = lax.optimization_barrier(jnp.max(scores, axis=-1, keepdims=True))
    weights = jnp.where(usable, jnp.exp(scores - peak_val), 0.0)
    totals = lax.optimization_barrier(jnp.sum(weights, axis=-1, keepdims=True))
    blended = jnp.einsum('bgrl,blgd->bgrd', rounded(weights), value_heads) / totals
    return blended.reshape(beam_count, -1)

def remote_attend(asked_query, page_data, length_now):
    child_count, new_count, query_width = asked_query.shape
    cache_len = page_data.shape[0]
    kv_width = page_data.shape[1] // 2
    kv_heads = kv_width // HD
    group_size = query_width // kv_width
    query_heads = asked_query.astype(jnp.float32).reshape(child_count, new_count, kv_heads, group_size, HD)
    key_heads = page_data[:, :kv_width].astype(jnp.float32).reshape(cache_len, kv_heads, HD)
    value_heads = page_data[:, kv_width:].astype(jnp.float32).reshape(cache_len, kv_heads, HD)
    scores = jnp.einsum('cngrd,lgd->cngrl', query_heads, key_heads) / math.sqrt(HD)
    usable = jnp.arange(cache_len, dtype=jnp.int32) < length_now
    scores = jnp.where(usable, scores, -1e+30)
    peak_val = lax.optimization_barrier(jnp.max(scores, axis=-1, keepdims=True))
    weights = jnp.where(usable, jnp.exp(scores - peak_val), 0.0)
    totals = lax.optimization_barrier(jnp.sum(weights, axis=-1, keepdims=True))
    blended = jnp.einsum('cngrl,lgd->cngrd', rounded(weights), value_heads) / totals
    log_total = peak_val[..., 0] + jnp.log(totals[..., 0])
    return (blended.reshape(child_count, new_count, query_width), log_total.reshape(child_count, new_count, -1))

def own_finish(asked_query, fresh_keyval, remote_out, log_total):
    child_count, new_count, query_width = asked_query.shape
    kv_width = fresh_keyval.shape[2] // 2
    kv_heads = kv_width // HD
    group_size = query_width // kv_width
    query_heads = asked_query.astype(jnp.float32).reshape(child_count, new_count, kv_heads, group_size, HD)
    key_heads = fresh_keyval[:, :, :kv_width].astype(jnp.float32).reshape(child_count, new_count, kv_heads, HD)
    value_heads = fresh_keyval[:, :, kv_width:].astype(jnp.float32).reshape(child_count, new_count, kv_heads, HD)
    scores = jnp.einsum('bngrd,bjgd->bngrj', query_heads, key_heads) / math.sqrt(HD)
    causal = jnp.arange(new_count)[None, :] <= jnp.arange(new_count)[:, None]
    causal = causal[None, :, None, None, :]
    scores = jnp.where(causal, scores, -1e+30)
    remote_log = log_total.reshape(child_count, new_count, kv_heads, group_size)
    peak_val = jnp.maximum(remote_log, lax.optimization_barrier(jnp.max(scores, axis=-1)))
    remote_weight = jnp.exp(remote_log - peak_val)
    weights = jnp.where(causal, jnp.exp(scores - peak_val[..., None]), 0.0)
    denominator = remote_weight + lax.optimization_barrier(jnp.sum(weights, axis=-1))
    own_part = jnp.einsum('bngrj,bjgd->bngrd', rounded(weights), value_heads)
    remote_heads = remote_out.reshape(child_count, new_count, kv_heads, group_size, HD)
    blended = (remote_weight[..., None] * remote_heads + own_part) / denominator[..., None]
    return blended.reshape(child_count, new_count, query_width).astype(jnp.bfloat16)

def reference(step_hidden, prm_cache, lengths, w_query, w_keyval, reward_head, placement, parents, page_table, policy_pool, new_query, new_keyval):
    normed = rms_rows(step_hidden)
    fresh_keyval = jnp.dot(normed, w_keyval, preferred_element_type=jnp.float32).astype(jnp.bfloat16)
    fresh_keyval = fresh_keyval.reshape(BEAMS, STEP, -1)
    last_rows = normed.reshape(BEAMS, STEP, -1)[:, STEP - 1]
    query_vec = jnp.dot(last_rows, w_query, preferred_element_type=jnp.float32).astype(jnp.bfloat16)
    blended = score_steps(query_vec, prm_cache, fresh_keyval, lengths)
    slot_reward = jnp.dot(blended, reward_head, precision=lax.Precision.HIGHEST)
    rewards = slot_reward[placement]

    def per_child(child):
        slot_now = parents[child]
        pool_rows = slot_now // B_DEV * (B_DEV * PPB) + page_table[slot_now]
        page_data = policy_pool[pool_rows].reshape(CTX, -1)
        asked_query = lax.dynamic_slice_in_dim(new_query, child, 1, 0)
        remote_out, log_total = remote_attend(asked_query, page_data, lengths[slot_now])
        return (remote_out[0], log_total[0])
    remote_out, log_total = lax.map(per_child, jnp.arange(BEAMS, dtype=jnp.int32))
    decoded = own_finish(new_query, new_keyval, remote_out, log_total)
    return (rewards, decoded)
```

```python
import functools
import math

import jax
import jax.numpy as jnp
from jax import lax
from jax.experimental import pallas as pl
from jax.experimental.pallas import tpu as pltpu
from jax.sharding import PartitionSpec as P

HQ = 16
HD = 128
EPS = 1e-05
SCALE = 1.0 / math.sqrt(HD)
LOW = -1e30


def dot_last(a, b):
    return lax.dot_general(a, b, (((1,), (1,)), ((), ())), preferred_element_type=jnp.float32)


def spread_heads(rows, mask):
    tiled = jnp.concatenate([rows] * (mask.shape[1] // HD), axis=1)
    return jnp.where(mask, tiled, jnp.zeros_like(tiled))


def exchange_kernel(
    n,
    src_child,
    row_slot,
    lengths,
    pages,
    own_dev,
    rows_ref,
    wq_ref,
    query_ref,
    keyval_ref,
    pool_ref,
    decoded_ref,
    q_ref,
    qsend,
    qrecv,
    rrecv,
    wq2,
    psend,
    precv,
    osend,
    orecv,
    lsend,
    lrecv,
    send_sem,
    recv_sem,
    wq_sem,
):
    me = lax.axis_index("fsdp")
    core = lax.rem(me, 2)
    sibling = me + 1 - 2 * core
    pair = lax.div(me, 2)
    barrier = pltpu.get_barrier_semaphore()
    half = wq2.shape[2]
    beams = query_ref.shape[0]

    def greet(k, c):
        pl.semaphore_signal(barrier, inc=1, device_id={"fsdp": lax.rem(me + k, n)})
        return c

    lax.fori_loop(1, n, greet, 0)

    def fill(j, c):
        qsend[j] = query_ref[src_child[j]]
        return c

    lax.fori_loop(0, n, fill, 0)
    pl.semaphore_wait(barrier, n - 1)

    def copy(lane, k, src, dst, sender_view=True):
        peer = lax.rem(me + k, n)
        return pltpu.make_async_remote_copy(
            src_ref=src,
            dst_ref=dst,
            send_sem=send_sem.at[lane, k],
            recv_sem=recv_sem.at[lane, k],
            device_id={"fsdp": peer},
        )

    def peer_of(k):
        return lax.rem(me + k, n)

    def rows_copy(k):
        return copy(0, k, rows_ref.at[lax.div(peer_of(k), 2)], rrecv.at[me])

    def q_copy(k):
        return copy(1, k, qsend.at[peer_of(k)], qrecv.at[me])

    def p_copy(k):
        return copy(2, k, psend.at[peer_of(k)], precv.at[me])

    def o_copy(k):
        return copy(3, k, osend.at[peer_of(k)], orecv.at[me])

    def l_copy(k):
        return copy(4, k, lsend.at[peer_of(k)], lrecv.at[me])

    def start_all(*makers):
        def body(k, c):
            for maker in makers:
                maker(k).start()
            return c

        lax.fori_loop(1, n, body, 0)

    def wait_all(*makers):
        def body(k, c):
            for maker in makers:
                maker(k).wait()
            return c

        lax.fori_loop(1, n, body, 0)

    wq_copy = pltpu.make_async_remote_copy(
        src_ref=wq_ref.at[:, pl.ds(pl.multiple_of((1 - core) * half, half), half)],
        dst_ref=wq2.at[core],
        send_sem=wq_sem.at[0],
        recv_sem=wq_sem.at[1],
        device_id={"fsdp": sibling},
    )
    wq_copy.start()
    start_all(rows_copy)
    start_all(q_copy)
    wq2[core] = wq_ref[:, pl.ds(pl.multiple_of(core * half, half), half)]
    rrecv[me] = rows_ref[pair]
    qrecv[me] = qsend[me]

    square = jnp.zeros((rows_ref.shape[1], 1), jnp.float32)
    for k in range(n // 2):
        part = rows_ref[k].astype(jnp.float32)
        square = square + jnp.sum(part * part, axis=1, keepdims=True)
    row_scale = lax.rsqrt(square / (rows_ref.shape[2] * (n // 2)) + EPS)

    wq_copy.wait()
    wait_all(rows_copy)
    depth = wq_ref.shape[0]
    arrived_rows = rrecv[...].reshape(n * rrecv.shape[1], rrecv.shape[2])
    weights_pair = wq2[...].reshape(2 * depth, half)
    step_cols = min(512, half)
    for c0 in range(0, half, step_cols):
        part = jnp.dot(
            arrived_rows, weights_pair[:, c0 : c0 + step_cols], preferred_element_type=jnp.float32
        ).astype(jnp.bfloat16)
        psend[:, :, c0 : c0 + step_cols] = part.reshape(n, rrecv.shape[1], step_cols)
    start_all(p_copy)
    precv[me] = psend[me]

    count = query_ref.shape[1]
    kv_width = pool_ref.shape[2] // 2
    row_id = lax.broadcasted_iota(jnp.int32, (count, kv_width), 0)
    col_id = lax.broadcasted_iota(jnp.int32, (count, kv_width), 1)
    group = HQ // (kv_width // HD)
    head_mask = (row_id % HQ) // group == col_id // HD
    row_small = lax.broadcasted_iota(jnp.int32, (count, HD), 0)
    col_small = lax.broadcasted_iota(jnp.int32, (count, HD), 1)
    eye = row_small == col_small
    kv_row = (row_small % HQ) // group

    wait_all(q_copy)
    page_rows = pool_ref.shape[1]
    token = lax.broadcasted_iota(jnp.int32, (count, 2 * page_rows), 1)

    def attend(i):
        slot = row_slot[i]
        first = pages[2 * slot]
        second = pages[2 * slot + 1]
        keys = jnp.concatenate([pool_ref[first, :, :kv_width], pool_ref[second, :, :kv_width]], axis=0)
        values = jnp.concatenate([pool_ref[first, :, kv_width:], pool_ref[second, :, kv_width:]], axis=0)
        s = dot_last(spread_heads(qrecv[i], head_mask), keys) * SCALE
        usable = token < lengths[slot]
        s = jnp.where(usable, s, LOW)
        peak = jnp.max(s, axis=1, keepdims=True)
        w = jnp.where(usable, jnp.exp(s - peak), 0.0)
        total = jnp.sum(w, axis=1, keepdims=True)
        wide = jnp.dot(w.astype(jnp.bfloat16), values, preferred_element_type=jnp.float32)
        wide = jnp.where(head_mask, wide, 0.0)
        out = wide[:, :HD]
        for g in range(1, kv_width // HD):
            out = out + wide[:, g * HD : (g + 1) * HD]
        osend[i] = (out / total).astype(jnp.bfloat16)
        log_total = peak + jnp.log(total)
        log_row = jnp.sum(jnp.where(eye, log_total, 0.0), axis=0, keepdims=True)
        lsend[i] = jnp.broadcast_to(log_row, (8, HD))

    def attend_four(b, c):
        for u in range(4):
            attend(b * 4 + u)
        return c

    lax.fori_loop(0, n // 4, attend_four, 0)
    start_all(l_copy, o_copy)
    orecv[me] = osend[me]
    lrecv[me] = lsend[me]
    wait_all(l_copy, o_copy)

    def finish(c):
        dev = own_dev[c]
        remote = orecv[dev].astype(jnp.float32)
        log_col = jnp.sum(jnp.where(eye, lrecv[dev][0:1, :], 0.0), axis=1, keepdims=True)
        q = query_ref[c].astype(jnp.float32)
        kv = keyval_ref[c].astype(jnp.float32)

        def expand(base):
            full = jnp.zeros((count, HD), jnp.float32)
            for g in range(kv_width // HD):
                full = jnp.where(kv_row == g, kv[base + g : base + g + 1, :], full)
            return full

        kv_heads = kv_width // HD
        scores = []
        for j in range(count // HQ):
            s = jnp.sum(q * expand(2 * j * kv_heads), axis=1, keepdims=True) * SCALE
            scores.append(jnp.where(row_small[:, :1] >= j * HQ, s, LOW))
        top = log_col
        for s in scores:
            top = jnp.maximum(top, s)
        weight = jnp.exp(log_col - top)
        acc = weight * remote
        den = weight
        for j, s in enumerate(scores):
            p = jnp.where(row_small[:, :1] >= j * HQ, jnp.exp(s - top), 0.0)
            den = den + p
            acc = acc + p.astype(jnp.bfloat16).astype(jnp.float32) * expand((2 * j + 1) * kv_heads)
        decoded_ref[c] = (acc / den).astype(jnp.bfloat16)

    def finish_four(b, c):
        for u in range(4):
            finish(b * 4 + u)
        return c

    lax.fori_loop(0, beams // 4, finish_four, 0)

    wait_all(p_copy)
    for side in range(2):
        total = precv[side].astype(jnp.float32)
        for k in range(1, n // 2):
            total = total + precv[2 * k + side].astype(jnp.float32)
        q_ref[:, side * half : (side + 1) * half] = (total * row_scale).astype(jnp.bfloat16)


def reward_kernel(
    n,
    lengths,
    place,
    hidden_ref,
    weights_ref,
    cache_ref,
    q_ref,
    head_ref,
    out_ref,
    fresh,
    cached_score,
    cached_value,
    qbd_all,
    mine,
    every,
    send_sem,
    recv_sem,
):
    me = lax.axis_index("fsdp")
    barrier = pltpu.get_barrier_semaphore()

    def greet(k, c):
        pl.semaphore_signal(barrier, inc=1, device_id={"fsdp": lax.rem(me + k, n)})
        return c

    lax.fori_loop(1, n, greet, 0)
    beams, cache_len, width = cache_ref.shape
    kv_width = width // 2
    group = HQ // (kv_width // HD)
    row_id = lax.broadcasted_iota(jnp.int32, (HQ, kv_width), 0)
    col_id = lax.broadcasted_iota(jnp.int32, (HQ, kv_width), 1)
    head_mask = row_id // group == col_id // HD
    token = lax.broadcasted_iota(jnp.int32, (HQ, cache_len), 1)

    def beam(b):
        q16 = q_ref[b]
        qbd = spread_heads(q16, head_mask)
        qbd_all[b] = qbd
        s = dot_last(qbd, cache_ref[b, :, :kv_width]) * SCALE
        cached_score[b] = jnp.where(token < lengths[b], s, LOW)
        v = dot_last(head_ref[...], cache_ref[b, :, kv_width:])
        cached_value[b] = v[:HQ] + v[HQ:]

    def beam_four(i, c):
        for u in range(4):
            beam(i * 4 + u)
        return c

    lax.fori_loop(0, beams // 4, beam_four, 0)

    row_count = hidden_ref.shape[0]
    block = row_count // 2

    def project(i, c):
        at = pl.ds(pl.multiple_of(i * block, block), block)
        x = hidden_ref[at, :]
        wide = x.astype(jnp.float32)
        scale = lax.rsqrt(jnp.mean(wide * wide, axis=1, keepdims=True) + EPS)
        fresh[at, :] = jnp.dot(x, weights_ref[...], preferred_element_type=jnp.float32) * scale
        return c

    lax.fori_loop(0, 2, project, 0)

    total_rows = beams * HQ
    step_len = row_count // beams
    fresh_keys = fresh[:, :kv_width].astype(jnp.bfloat16)
    sf = dot_last(qbd_all[...].reshape(total_rows, kv_width), fresh_keys) * SCALE
    r = lax.broadcasted_iota(jnp.int32, (total_rows, row_count), 0)
    k = lax.broadcasted_iota(jnp.int32, (total_rows, row_count), 1)
    same = r // HQ == k // step_len
    sf = jnp.where(same, sf, LOW)
    sc = cached_score[...].reshape(total_rows, cache_len)
    peak = jnp.maximum(jnp.max(sf, axis=1, keepdims=True), jnp.max(sc, axis=1, keepdims=True))
    wf = jnp.where(same, jnp.exp(sf - peak), 0.0)
    wc = jnp.where(sc > 0.5 * LOW, jnp.exp(sc - peak), 0.0)
    vt = jnp.transpose(fresh[:, kv_width : kv_width + HD])
    vf = vt[:HQ] + vt[HQ : 2 * HQ]
    vf = jnp.broadcast_to(vf[None], (beams, HQ, row_count)).reshape(total_rows, row_count)
    vc = cached_value[...].reshape(total_rows, cache_len)
    den = jnp.sum(wf, axis=1, keepdims=True) + jnp.sum(wc, axis=1, keepdims=True)
    num = jnp.sum(wf * vf, axis=1, keepdims=True) + jnp.sum(wc * vc, axis=1, keepdims=True)
    ratio = num / den
    rr = lax.broadcasted_iota(jnp.int32, (total_rows, HD), 0)
    cc = lax.broadcasted_iota(jnp.int32, (total_rows, HD), 1)
    row = jnp.sum(jnp.where(rr // HQ == cc, ratio, 0.0), axis=0, keepdims=True)
    mine[...] = jnp.broadcast_to(row, (8, HD))
    every[me] = mine[...]

    pl.semaphore_wait(barrier, n - 1)

    def copy(k):
        return pltpu.make_async_remote_copy(
            src_ref=mine,
            dst_ref=every.at[me],
            send_sem=send_sem.at[k],
            recv_sem=recv_sem.at[k],
            device_id={"fsdp": lax.rem(me + k, n)},
        )

    def start(k, c):
        copy(k).start()
        return c

    def wait(k, c):
        copy(k).wait()
        return c

    lax.fori_loop(1, n, start, 0)
    lax.fori_loop(1, n, wait, 0)
    lane = lax.broadcasted_iota(jnp.int32, (1, HD), 1)
    for b in range(beams):
        spot = place[b]
        got = every[lax.div(spot, beams)][0:1, :]
        out_ref[b : b + 1, :] = jnp.broadcast_to(
            jnp.sum(jnp.where(lane == lax.rem(spot, beams), got, 0.0), axis=1, keepdims=True), (1, HD)
        )


def split_two(x):
    high = x.astype(jnp.bfloat16)
    return high, (x - high.astype(jnp.float32)).astype(jnp.bfloat16)


def shards(
    step_hidden,
    prm_cache,
    lengths,
    w_query,
    w_keyval,
    reward_head,
    placement,
    parents,
    page_table,
    policy_pool,
    new_query,
    new_keyval,
):
    me = lax.axis_index("fsdp")
    n = lax.axis_size("fsdp")
    beams = lengths.shape[0]
    step_len = step_hidden.shape[0] // beams
    width = step_hidden.shape[1]
    kv_width = w_keyval.shape[1] // 2
    kv_heads = kv_width // HD
    group = HQ // kv_heads
    depth = w_query.shape[0]
    half = w_query.shape[1] // 2
    new = new_query.shape[1]
    bf16, f32 = jnp.bfloat16, jnp.float32

    head_rows = reward_head.reshape(HQ, HD)
    head_mask = (jnp.arange(HQ)[:, None] // group) == (jnp.arange(kv_width)[None, :] // HD)
    head_wide = jnp.where(head_mask, jnp.tile(head_rows, (1, kv_heads)), 0.0)
    head_two = jnp.concatenate(split_two(head_wide), axis=0)
    folded = dot_last(w_keyval[:, kv_width:], head_two)
    folded = folded[:, :HQ] + folded[:, HQ:]
    pieces = split_two(folded)
    own_weights = jnp.concatenate(
        [w_keyval[:, :kv_width], pieces[0], pieces[1], jnp.zeros((depth, HD - 2 * HQ), bf16)], axis=1
    )
    weights = lax.all_gather(own_weights, "fsdp", axis=0, tiled=True)

    last = step_hidden.reshape(beams, step_len, width)[:, step_len - 1]
    rows = last.reshape(beams, n // 2, 2 * depth).transpose(1, 0, 2)
    parent_dev = parents // beams
    parent_inner = parents % beams
    serves = parent_dev.reshape(n, beams) == me
    row_slot = jnp.sum(jnp.where(serves, parent_inner.reshape(n, beams), 0), axis=1)
    own_dev = lax.dynamic_slice_in_dim(parent_dev, me * beams, beams)
    chosen = jnp.arange(n, dtype=jnp.int32)[:, None] == own_dev[None, :]
    src_child = jnp.sum(jnp.where(chosen, jnp.arange(beams, dtype=jnp.int32)[None, :], 0), axis=1)

    smem = pl.BlockSpec(memory_space=pltpu.SMEM)
    vmem = pl.BlockSpec(memory_space=pltpu.VMEM)
    count = new * HQ
    decoded, q = pl.pallas_call(
        functools.partial(exchange_kernel, n),
        out_shape=(
            jax.ShapeDtypeStruct((beams, count, HD), bf16),
            jax.ShapeDtypeStruct((beams, 2 * half), bf16),
        ),
        in_specs=[smem] * 5 + [vmem] * 5,
        out_specs=(vmem, vmem),
        scratch_shapes=[
            pltpu.VMEM((n, count, HD), bf16),
            pltpu.VMEM((n, count, HD), bf16),
            pltpu.VMEM((n, beams, 2 * depth), bf16),
            pltpu.VMEM((2, depth, half), bf16),
            pltpu.VMEM((n, beams, half), bf16),
            pltpu.VMEM((n, beams, half), bf16),
            pltpu.VMEM((n, count, HD), bf16),
            pltpu.VMEM((n, count, HD), bf16),
            pltpu.VMEM((n, 8, HD), f32),
            pltpu.VMEM((n, 8, HD), f32),
            pltpu.SemaphoreType.DMA((5, n)),
            pltpu.SemaphoreType.DMA((5, n)),
            pltpu.SemaphoreType.DMA((2,)),
        ],
        compiler_params=pltpu.CompilerParams(
            collective_id=0, has_side_effects=True, vmem_limit_bytes=28 * 2**20
        ),
        cost_estimate=pl.CostEstimate(flops=10**9, bytes_accessed=8 * 2**20, transcendentals=0),
    )(
        src_child,
        row_slot,
        lengths,
        page_table.reshape(-1),
        own_dev,
        rows,
        w_query,
        new_query.reshape(beams, count, HD),
        new_keyval.reshape(beams, new * 2 * kv_heads, HD),
        policy_pool,
    )

    my_place = lax.dynamic_slice_in_dim(placement, me * beams, beams)
    cache_len = prm_cache.shape[1]
    rewards = pl.pallas_call(
        functools.partial(reward_kernel, n),
        out_shape=jax.ShapeDtypeStruct((beams, HD), f32),
        in_specs=[smem] * 2 + [vmem] * 5,
        out_specs=vmem,
        scratch_shapes=[
            pltpu.VMEM((beams * step_len, kv_width + HD), f32),
            pltpu.VMEM((beams, HQ, cache_len), f32),
            pltpu.VMEM((beams, HQ, cache_len), f32),
            pltpu.VMEM((beams, HQ, kv_width), bf16),
            pltpu.VMEM((8, HD), f32),
            pltpu.VMEM((n, 8, HD), f32),
            pltpu.SemaphoreType.DMA((n,)),
            pltpu.SemaphoreType.DMA((n,)),
        ],
        compiler_params=pltpu.CompilerParams(
            collective_id=1, has_side_effects=True, vmem_limit_bytes=36 * 2**20
        ),
        cost_estimate=pl.CostEstimate(flops=3 * 10**9, bytes_accessed=14 * 2**20, transcendentals=0),
    )(lengths, my_place, step_hidden, weights, prm_cache, q.reshape(beams, HQ, HD), head_two)
    return (rewards[:, 0], decoded.reshape(beams, new, HQ * HD))


def solution(mesh):
    in_specs = (
        P(("groups", "fsdp"), None),
        P(("groups", "fsdp"), None, None),
        P(("groups", "fsdp")),
        P("fsdp", None),
        P("fsdp", None),
        P(),
        P("groups"),
        P("groups"),
        P(("groups", "fsdp"), None),
        P(("groups", "fsdp"), None, None),
        P(("groups", "fsdp"), None, None),
        P(("groups", "fsdp"), None, None),
    )
    out_specs = (P(("groups", "fsdp")), P(("groups", "fsdp"), None, None))
    return jax.shard_map(shards, mesh=mesh, in_specs=in_specs, out_specs=out_specs, check_vma=False)
```

```python
import functools
import math

import jax
import jax.numpy as jnp
from jax import lax
from jax.experimental import pallas as pl
from jax.experimental.pallas import tpu as pltpu
from jax.sharding import PartitionSpec as P

HQ = 16
HD = 128
EPS = 1e-05
SCALE = 1.0 / math.sqrt(HD)
LOW = -1e30


def dot_last(a, b):
    return lax.dot_general(a, b, (((1,), (1,)), ((), ())), preferred_element_type=jnp.float32)


def spread_heads(rows, mask):
    tiled = jnp.concatenate([rows] * (mask.shape[1] // HD), axis=1)
    return jnp.where(mask, tiled, jnp.zeros_like(tiled))


def score_kernel(
    n,
    lengths,
    pages,
    place,
    parents,
    rows_ref,
    wq_ref,
    wkv_ref,
    head_ref,
    query_ref,
    keyval_ref,
    hidden_hbm,
    cache_hbm,
    pool_hbm,
    decoded_ref,
    out_ref,
    hidden_ref,
    cache_ref,
    pool_ref,
    weights,
    fresh,
    cached_score,
    cached_value,
    qbd_all,
    q_heads,
    mine,
    every,
    qsend,
    qrecv,
    rrecv,
    wq2,
    psend,
    precv,
    osend,
    orecv,
    lsend,
    lrecv,
    send_sem,
    recv_sem,
    wq_sem,
    z_sem,
    y_sem,
    c_sem,
    load_sem,
):
    me = lax.axis_index("fsdp")
    core = lax.rem(me, 2)
    sibling = me + 1 - 2 * core
    pair = lax.div(me, 2)
    across = me + 2 - 4 * lax.rem(pair, 2)
    low = lax.rem(me, 4)
    column = lax.div(me, 4)
    columns = n // 4
    barrier = pltpu.get_barrier_semaphore()
    half = wq2.shape[2]
    beams = query_ref.shape[0]
    depth = wq_ref.shape[0]

    def greet(k, c):
        pl.semaphore_signal(barrier, inc=1, device_id={"fsdp": lax.rem(me + k, n)})
        return c

    lax.fori_loop(1, n, greet, 0)

    loads = [
        pltpu.make_async_copy(src, dst, load_sem.at[i])
        for i, (src, dst) in enumerate(
            [(pool_hbm, pool_ref), (cache_hbm, cache_ref), (hidden_hbm, hidden_ref)]
        )
    ]
    for load in loads:
        load.start()

    def fill(j, c):
        pick = jnp.int32(0)
        for child in range(beams):
            hit = lax.div(parents[me * beams + child], beams) == j
            pick = jnp.maximum(pick, jnp.where(hit, child, 0))
        qsend[j] = query_ref[pick]
        return c

    lax.fori_loop(0, n, fill, 0)

    def peer_of(k):
        return lax.rem(me + k, n)

    def copy(lane, k, src, dst):
        return pltpu.make_async_remote_copy(
            src_ref=src,
            dst_ref=dst,
            send_sem=send_sem.at[lane, k],
            recv_sem=recv_sem.at[lane, k],
            device_id={"fsdp": peer_of(k)},
        )

    def rows_copy(k):
        return copy(0, k, rows_ref.at[lax.div(peer_of(k), 2)], rrecv.at[me])

    def q_copy(k):
        return copy(1, k, qsend.at[peer_of(k)], qrecv.at[me])

    def p_copy(k):
        return copy(2, k, psend.at[peer_of(k)], precv.at[me])

    def o_copy(k):
        return copy(3, k, osend.at[peer_of(k)], orecv.at[me])

    def l_copy(k):
        return copy(4, k, lsend.at[peer_of(k)], lrecv.at[me])

    def reward_copy(k):
        return copy(5, k, mine, every.at[me])

    def start_all(*makers):
        def body(k, c):
            for maker in makers:
                maker(k).start()
            return c

        lax.fori_loop(1, n, body, 0)

    def wait_all(*makers):
        def body(k, c):
            for maker in makers:
                maker(k).wait()
            return c

        lax.fori_loop(1, n, body, 0)

    def block_of(k, member):
        return lax.rem(column + columns - k, columns) * 4 + member

    def z_copy(k):
        return pltpu.make_async_remote_copy(
            src_ref=weights.at[me],
            dst_ref=weights.at[me],
            send_sem=z_sem.at[0, k],
            recv_sem=z_sem.at[1, k],
            device_id={"fsdp": lax.rem(column + k, columns) * 4 + low},
        )

    def y_copy(k):
        block = block_of(k, low)
        return pltpu.make_async_remote_copy(
            src_ref=weights.at[block],
            dst_ref=weights.at[block],
            send_sem=y_sem.at[0, k],
            recv_sem=y_sem.at[1, k],
            device_id={"fsdp": across},
        )

    def c_copy(side, k):
        block = block_of(k, low if side == 0 else lax.rem(low + 2, 4))
        return pltpu.make_async_remote_copy(
            src_ref=weights.at[block],
            dst_ref=weights.at[block],
            send_sem=c_sem.at[0, side, k],
            recv_sem=c_sem.at[1, side, k],
            device_id={"fsdp": sibling},
        )

    wq_copy = pltpu.make_async_remote_copy(
        src_ref=wq_ref.at[:, pl.ds(pl.multiple_of((1 - core) * half, half), half)],
        dst_ref=wq2.at[core],
        send_sem=wq_sem.at[0],
        recv_sem=wq_sem.at[1],
        device_id={"fsdp": sibling},
    )
    pl.semaphore_wait(barrier, n - 1)
    wq_copy.start()
    start_all(rows_copy)
    start_all(q_copy)

    beam_count, cache_len, width = cache_ref.shape
    kv_width = width // 2
    kv_heads = kv_width // HD
    group = HQ // kv_heads
    folded = dot_last(wkv_ref[:, kv_width:], head_ref[...])
    folded = folded + pltpu.roll(folded, HD - HQ, 1)
    high = folded.astype(jnp.bfloat16).astype(jnp.float32)
    lane_w = lax.broadcasted_iota(jnp.int32, (depth, HD), 1)
    rest = pltpu.roll(folded - high, HQ, 1)
    both = jnp.where(lane_w < HQ, high, jnp.where(lane_w < 2 * HQ, rest, 0.0))
    weights[me, :, :kv_width] = wkv_ref[:, :kv_width]
    weights[me, :, kv_width:] = both.astype(jnp.bfloat16)

    def z_start(k, c):
        z_copy(k).start()
        return c

    lax.fori_loop(1, columns, z_start, 0)
    y_copy(0).start()
    c_copy(0, 0).start()

    wq2[core] = wq_ref[:, pl.ds(pl.multiple_of(core * half, half), half)]
    rrecv[me] = rows_ref[pair]
    qrecv[me] = qsend[me]
    square = jnp.zeros((rows_ref.shape[1], 1), jnp.float32)
    for k in range(n // 2):
        part = rows_ref[k].astype(jnp.float32)
        square = square + jnp.sum(part * part, axis=1, keepdims=True)
    row_scale = lax.rsqrt(square / (rows_ref.shape[2] * (n // 2)) + EPS)

    wq_copy.wait()
    wait_all(rows_copy)
    arrived_rows = rrecv[...].reshape(n * rrecv.shape[1], rrecv.shape[2])
    weights_pair = wq2[...].reshape(2 * depth, half)
    step_cols = min(512, half)
    for c0 in range(0, half, step_cols):
        part = jnp.dot(
            arrived_rows, weights_pair[:, c0 : c0 + step_cols], preferred_element_type=jnp.float32
        ).astype(jnp.bfloat16)
        psend[:, :, c0 : c0 + step_cols] = part.reshape(n, rrecv.shape[1], step_cols)
    start_all(p_copy)
    precv[me] = psend[me]

    count = query_ref.shape[1]
    row_id = lax.broadcasted_iota(jnp.int32, (count, kv_width), 0)
    col_id = lax.broadcasted_iota(jnp.int32, (count, kv_width), 1)
    head_mask = (row_id % HQ) // group == col_id // HD
    row_small = lax.broadcasted_iota(jnp.int32, (count, HD), 0)
    col_small = lax.broadcasted_iota(jnp.int32, (count, HD), 1)
    eye = row_small == col_small
    kv_row = (row_small % HQ) // group

    loads[0].wait()
    wait_all(q_copy)
    page_rows = pool_ref.shape[1]
    token = lax.broadcasted_iota(jnp.int32, (count, 2 * page_rows), 1)

    def attend(i):
        slot = jnp.int32(0)
        for child in range(beams):
            parent = parents[i * beams + child]
            inner = lax.rem(parent, beams)
            slot = jnp.maximum(slot, jnp.where(lax.div(parent, beams) == me, inner, 0))
        first = pages[slot, 0]
        second = pages[slot, 1]
        keys = jnp.concatenate([pool_ref[first, :, :kv_width], pool_ref[second, :, :kv_width]], axis=0)
        values = jnp.concatenate([pool_ref[first, :, kv_width:], pool_ref[second, :, kv_width:]], axis=0)
        s = dot_last(spread_heads(qrecv[i], head_mask), keys) * SCALE
        usable = token < lengths[slot]
        s = jnp.where(usable, s, LOW)
        peak = jnp.max(s, axis=1, keepdims=True)
        w = jnp.where(usable, jnp.exp(s - peak), 0.0)
        total = jnp.sum(w, axis=1, keepdims=True)
        wide = jnp.dot(w.astype(jnp.bfloat16), values, preferred_element_type=jnp.float32)
        wide = jnp.where(head_mask, wide, 0.0)
        out = wide[:, :HD]
        for g in range(1, kv_heads):
            out = out + wide[:, g * HD : (g + 1) * HD]
        osend[i] = (out / total).astype(jnp.bfloat16)
        log_total = peak + jnp.log(total)
        log_row = jnp.sum(jnp.where(eye, log_total, 0.0), axis=0, keepdims=True)
        lsend[i] = jnp.broadcast_to(log_row, (8, HD))

    def attend_four(b, c):
        for u in range(4):
            attend(b * 4 + u)
        return c

    lax.fori_loop(0, n // 4, attend_four, 0)
    start_all(l_copy, o_copy)
    orecv[me] = osend[me]
    lrecv[me] = lsend[me]

    def z_pass(k, c):
        z_copy(k).wait()
        y_copy(k).start()
        c_copy(0, k).start()
        return c

    lax.fori_loop(1, columns, z_pass, 0)

    loads[1].wait()

    def cache_value(b, c):
        for u in range(4):
            v = dot_last(head_ref[: 2 * HQ, :], cache_ref[b * 4 + u, :, kv_width:])
            cached_value[b * 4 + u] = v[:HQ] + v[HQ : 2 * HQ]
        return c

    lax.fori_loop(0, beam_count // 4, cache_value, 0)
    wait_all(l_copy, o_copy)

    def finish(c):
        dev = lax.div(parents[me * beams + c], beams)
        remote = orecv[dev].astype(jnp.float32)
        log_col = jnp.sum(jnp.where(eye, lrecv[dev][0:1, :], 0.0), axis=1, keepdims=True)
        q = query_ref[c].astype(jnp.float32)
        kv = keyval_ref[c].astype(jnp.float32)

        def expand(base):
            full = jnp.zeros((count, HD), jnp.float32)
            for g in range(kv_heads):
                full = jnp.where(kv_row == g, kv[base + g : base + g + 1, :], full)
            return full

        scores = []
        for j in range(count // HQ):
            s = jnp.sum(q * expand(2 * j * kv_heads), axis=1, keepdims=True) * SCALE
            scores.append(jnp.where(row_small[:, :1] >= j * HQ, s, LOW))
        top = log_col
        for s in scores:
            top = jnp.maximum(top, s)
        weight = jnp.exp(log_col - top)
        acc = weight * remote
        den = weight
        for j, s in enumerate(scores):
            p = jnp.where(row_small[:, :1] >= j * HQ, jnp.exp(s - top), 0.0)
            den = den + p
            acc = acc + p.astype(jnp.bfloat16).astype(jnp.float32) * expand((2 * j + 1) * kv_heads)
        decoded_ref[c] = (acc / den).astype(jnp.bfloat16)

    def finish_four(b, c):
        for u in range(4):
            finish(b * 4 + u)
        return c

    lax.fori_loop(0, beams // 4, finish_four, 0)

    def y_pass(k, c):
        y_copy(k).wait()
        c_copy(1, k).start()
        return c

    lax.fori_loop(0, columns, y_pass, 0)

    wait_all(p_copy)
    for side in range(2):
        total = precv[side].astype(jnp.float32)
        for k in range(1, n // 2):
            total = total + precv[2 * k + side].astype(jnp.float32)
        total = (total * row_scale).astype(jnp.bfloat16).astype(jnp.float32)
        for h in range(half // HD):
            q_heads[:, side * (half // HD) + h, :] = total[:, h * HD : (h + 1) * HD]

    mask16 = head_mask[:HQ]
    token16 = lax.broadcasted_iota(jnp.int32, (HQ, cache_len), 1)

    def cache_scores(i, c):
        for u in range(4):
            b = i * 4 + u
            qbd = spread_heads(q_heads[b].astype(jnp.bfloat16), mask16)
            qbd_all[b] = qbd
            s = dot_last(qbd, cache_ref[b, :, :kv_width]) * SCALE
            cached_score[b] = jnp.where(token16 < lengths[b], s, LOW)
        return c

    lax.fori_loop(0, beam_count // 4, cache_scores, 0)

    loads[2].wait()

    def c_pass(k, c):
        c_copy(0, k).wait()
        c_copy(1, k).wait()
        return c

    lax.fori_loop(0, columns, c_pass, 0)

    row_count = hidden_ref.shape[0]
    block = row_count // 2
    depth_all = n * depth

    def project(i, c):
        at = pl.ds(pl.multiple_of(i * block, block), block)
        x = hidden_ref[at, :]
        wide = x.astype(jnp.float32)
        scale = lax.rsqrt(jnp.mean(wide * wide, axis=1, keepdims=True) + EPS)
        w_all = weights[...].reshape(depth_all, weights.shape[2])
        fresh[at, :] = jnp.dot(x, w_all, preferred_element_type=jnp.float32) * scale
        return c

    lax.fori_loop(0, 2, project, 0)

    total_rows = beams * HQ
    step_len = row_count // beams
    fresh_keys = fresh[:, :kv_width].astype(jnp.bfloat16)
    sf = dot_last(qbd_all[...].reshape(total_rows, kv_width), fresh_keys) * SCALE
    r = lax.broadcasted_iota(jnp.int32, (total_rows, row_count), 0)
    k = lax.broadcasted_iota(jnp.int32, (total_rows, row_count), 1)
    same = r // HQ == k // step_len
    sf = jnp.where(same, sf, LOW)
    sc = cached_score[...].reshape(total_rows, cache_len)
    peak = jnp.maximum(jnp.max(sf, axis=1, keepdims=True), jnp.max(sc, axis=1, keepdims=True))
    wf = jnp.where(same, jnp.exp(sf - peak), 0.0)
    wc = jnp.where(sc > 0.5 * LOW, jnp.exp(sc - peak), 0.0)
    vt = jnp.transpose(fresh[:, kv_width : kv_width + HD])
    vf = vt[:HQ] + vt[HQ : 2 * HQ]
    vf = jnp.broadcast_to(vf[None], (beams, HQ, row_count)).reshape(total_rows, row_count)
    vc = cached_value[...].reshape(total_rows, cache_len)
    den = jnp.sum(wf, axis=1, keepdims=True) + jnp.sum(wc, axis=1, keepdims=True)
    num = jnp.sum(wf * vf, axis=1, keepdims=True) + jnp.sum(wc * vc, axis=1, keepdims=True)
    ratio = num / den
    rr = lax.broadcasted_iota(jnp.int32, (total_rows, HD), 0)
    cc = lax.broadcasted_iota(jnp.int32, (total_rows, HD), 1)
    row = jnp.sum(jnp.where(rr // HQ == cc, ratio, 0.0), axis=0, keepdims=True)
    mine[...] = jnp.broadcast_to(row, (8, HD))
    every[me] = mine[...]
    start_all(reward_copy)
    wait_all(reward_copy)
    lane = lax.broadcasted_iota(jnp.int32, (1, HD), 1)
    for b in range(beams):
        spot = place[me * beams + b]
        got = every[lax.div(spot, beams)][0:1, :]
        out_ref[b : b + 1, :] = jnp.broadcast_to(
            jnp.sum(jnp.where(lane == lax.rem(spot, beams), got, 0.0), axis=1, keepdims=True), (1, HD)
        )


def split_two(x):
    high = x.astype(jnp.bfloat16)
    return high, (x - high.astype(jnp.float32)).astype(jnp.bfloat16)


def shards(
    step_hidden,
    prm_cache,
    lengths,
    w_query,
    w_keyval,
    reward_head,
    placement,
    parents,
    page_table,
    policy_pool,
    new_query,
    new_keyval,
):
    n = lax.axis_size("fsdp")
    beams, cache_len, _ = prm_cache.shape
    row_count, width = step_hidden.shape
    step_len = row_count // beams
    kv_width = w_keyval.shape[1] // 2
    kv_heads = kv_width // HD
    group = HQ // kv_heads
    depth = w_query.shape[0]
    half = w_query.shape[1] // 2
    new = new_query.shape[1]
    count = new * HQ
    bf16, f32 = jnp.bfloat16, jnp.float32

    head_mask = (jnp.arange(HQ)[:, None] // group) == (jnp.arange(kv_width)[None, :] // HD)
    head_wide = jnp.where(head_mask, jnp.tile(reward_head.reshape(HQ, HD), (1, kv_heads)), 0.0)
    head_two = jnp.concatenate(
        (*split_two(head_wide), jnp.zeros((HD - 2 * HQ, kv_width), bf16)), axis=0
    )
    last = step_hidden.reshape(beams, step_len, width)[:, step_len - 1]
    rows = last.reshape(beams, n // 2, 2 * depth).transpose(1, 0, 2)

    smem = pl.BlockSpec(memory_space=pltpu.SMEM)
    vmem = pl.BlockSpec(memory_space=pltpu.VMEM)
    hbm = pl.BlockSpec(memory_space=pl.ANY)
    dma = pltpu.SemaphoreType.DMA
    decoded, rewards = pl.pallas_call(
        functools.partial(score_kernel, n),
        out_shape=(
            jax.ShapeDtypeStruct((beams, count, HD), bf16),
            jax.ShapeDtypeStruct((beams, HD), f32),
        ),
        in_specs=[smem] * 4 + [vmem] * 6 + [hbm] * 3,
        out_specs=(vmem, vmem),
        scratch_shapes=[
            pltpu.VMEM(step_hidden.shape, bf16),
            pltpu.VMEM(prm_cache.shape, bf16),
            pltpu.VMEM(policy_pool.shape, bf16),
            pltpu.VMEM((n, depth, kv_width + HD), bf16),
            pltpu.VMEM((row_count, kv_width + HD), f32),
            pltpu.VMEM((beams, HQ, cache_len), f32),
            pltpu.VMEM((beams, HQ, cache_len), f32),
            pltpu.VMEM((beams, HQ, kv_width), bf16),
            pltpu.VMEM((beams, HQ, HD), f32),
            pltpu.VMEM((8, HD), f32),
            pltpu.VMEM((n, 8, HD), f32),
            pltpu.VMEM((n, count, HD), bf16),
            pltpu.VMEM((n, count, HD), bf16),
            pltpu.VMEM((n, beams, 2 * depth), bf16),
            pltpu.VMEM((2, depth, half), bf16),
            pltpu.VMEM((n, beams, half), bf16),
            pltpu.VMEM((n, beams, half), bf16),
            pltpu.VMEM((n, count, HD), bf16),
            pltpu.VMEM((n, count, HD), bf16),
            pltpu.VMEM((n, 8, HD), f32),
            pltpu.VMEM((n, 8, HD), f32),
            dma((6, n)),
            dma((6, n)),
            dma((2,)),
            dma((2, n // 4)),
            dma((2, n // 4)),
            dma((2, 2, n // 4)),
            dma((3,)),
        ],
        compiler_params=pltpu.CompilerParams(
            collective_id=0, has_side_effects=True, vmem_limit_bytes=52 * 2**20
        ),
        cost_estimate=pl.CostEstimate(
            flops=4 * 10**9, bytes_accessed=20 * 2**20, transcendentals=0
        ),
    )(
        lengths,
        page_table,
        placement,
        parents,
        rows,
        w_query,
        w_keyval,
        head_two,
        new_query.reshape(beams, count, HD),
        new_keyval.reshape(beams, new * 2 * kv_heads, HD),
        step_hidden,
        prm_cache,
        policy_pool,
    )
    return (rewards[:, 0], decoded.reshape(beams, new, HQ * HD))


def solution(mesh):
    in_specs = (
        P(("groups", "fsdp"), None),
        P(("groups", "fsdp"), None, None),
        P(("groups", "fsdp")),
        P("fsdp", None),
        P("fsdp", None),
        P(),
        P("groups"),
        P("groups"),
        P(("groups", "fsdp"), None),
        P(("groups", "fsdp"), None, None),
        P(("groups", "fsdp"), None, None),
        P(("groups", "fsdp"), None, None),
    )
    out_specs = (P(("groups", "fsdp")), P(("groups", "fsdp"), None, None))
    return jax.shard_map(shards, mesh=mesh, in_specs=in_specs, out_specs=out_specs, check_vma=False)
```
